32 devices in a mesh: sec: 2 (over x), dev: 8 (over z, y), rep: 2 (over core).
Axes of the slice: x: 2, y: 2, z: 4, core: 2. Of those that a mesh axis runs over, the one named last changes fastest.
Arguments:
- resid: bfloat16 [2048, 4096], P(('rep', 'dev')), parts along dimension 0, may hold values from -27 to 27
- queries: bfloat16 [2048, 4096], P(('rep', 'dev'), 'sec'), parts along dimension 0, may hold values from -30 to 30
- keys: bfloat16 [2048, 1024], P(('rep', 'dev'), 'sec'), parts along dimension 0, may hold values from -6 to 6
- values: bfloat16 [2048, 1024], P(('rep', 'dev'), 'sec'), parts along dimension 0, may hold values from -6 to 6
- norm_gain: float32 [4096], replicated, may hold values from 0.1 to 1.9
- expert_ids: int32 [2048, 2], P(('rep', 'dev')), parts along dimension 0, may hold values from 0 to 3, all different within a row; in each aligned block of 128 rows (0 to 127, 128 to 255, ...) at most 80 rows name the same one
- gate_weights: float32 [2048, 2], P(('rep', 'dev')), parts along dimension 0, may hold values from 0.2 to 1
- w_gate: bfloat16 [8, 4096, 768], P('dev', None, 'sec'), may hold values from -0.09375 to 0.09375
- w_up: bfloat16 [8, 4096, 768], P('dev', None, 'sec'), may hold values from -0.09375 to 0.09375
- w_down: bfloat16 [8, 768, 4096], P('dev', 'sec'), may hold values from -0.15625 to 0.15625
Outputs:
- out: bfloat16 [2048, 4096], P(('rep', 'dev'), 'sec'), parts along dimension 0
The draws below stay inside these ranges and needn't reach their ends.
There are 2 independent parts, one for each index of `rep`. The reference program is written for one: setup_inputs(seed, part) draws one part's arguments, and reference() takes and returns one part's arrays. A program takes and returns all parts, laid end to end along the dimension named above; an argument that names none is the same for every part. Nothing has to cross between parts.
Inputs may be any that keep to these rules, and one draw needn't show every extreme that they name: `expert_ids`: each token names 2 different experts; among the tokens of one index of dev no expert is named more than 80 times.
All inputs are finite; a program needn't handle non-finite values.
Results may differ from the reference program's by a relative error of at most 0.008.
Values may be sent and summed in bfloat16 or wider, within the bound.
No kernel may reach another device: no remote copies, remote signals or barrier semaphores. Data moves between devices by JAX's collectives and lax.ppermute only.
A program may use at most 128 MiB of HBM per device.

```python
import math
import jax
import jax.numpy as jnp
import numpy as np
from jax import lax

D = 4096
HEADS = 32
KV = 8
HD = 128
FF = 1536
TOPK = 2
TOK_DEV = 128
TOKENS = 1024
EXPERTS = 4
CAP = 80
N_DEV = 8


def draw_keys(key, part):
    noise_key = jax.random.fold_in(key, 23)
    result = jnp.clip(jax.random.normal(noise_key, (TOKENS, KV, HD), jnp.float32), -6.0, 6.0)
    return result.reshape(TOKENS, KV * HD).astype(jnp.bfloat16)


def draw_queries(key, part):
    noise_key = jax.random.fold_in(key, 29)
    group_size = HEADS // KV
    result = jnp.clip(3.0 * jax.random.normal(noise_key, (TOKENS, KV, group_size, HD), jnp.float32), -12.0, 12.0)
    return result.reshape(TOKENS, HEADS * HD).astype(jnp.bfloat16)


def draw_resid(key, part):
    base_key = jax.random.fold_in(key, 31)
    noise_key, row_key, column_key = jax.random.split(base_key, 3)
    low_log = math.log(0.3)
    high_log = math.log(3.0)
    row_scale = jnp.exp(jax.random.uniform(row_key, (TOKENS, 1), jnp.float32, low_log, high_log))
    column_scale = jnp.exp(jax.random.uniform(column_key, (1, D), jnp.float32, low_log, high_log))
    base_draw = jnp.clip(jax.random.normal(noise_key, (TOKENS, D), jnp.float32), -3.0, 3.0)
    return (base_draw * row_scale * column_scale).astype(jnp.bfloat16)


def steps_of(key, shape, cuts, smallest, top_value):
    factor_of = 1.0
    for position, parts in cuts:
        draws = jax.random.uniform(jax.random.fold_in(jax.random.fold_in(key, 6), position), (parts,), jnp.float32, smallest / len(cuts), top_value / len(cuts))
        factor_of = factor_of * jnp.repeat(jnp.exp(draws), shape[position] // parts).reshape((-1,) + (1,) * (len(shape) - 1 - position))
    return factor_of


def deal_out(own_key, own, number, rows, count, top, reach, skew):
    order = jax.random.permutation(own_key, count)
    packed, ordinary = portions_of(count, rows * top, reach, skew, True), portions_of(count, rows * top, reach, skew, False)
    places = jnp.arange(count)

    def named(lengths, turn):
        used = int((lengths > 0).sum())
        fixed = max(1, used // 4)
        moved = fixed + (places - fixed + turn * (used - fixed)) % max(1, count - fixed)
        return jnp.zeros((count,), jnp.int32).at[order[jnp.where(places < fixed, places, moved)]].set(jnp.asarray(lengths, jnp.int32))

    lengths = jnp.where(number % 4 == 0, named(packed, number // 4), named(ordinary, number - number // 4 - 1))
    mixed = jax.random.permutation(jax.random.fold_in(own, 3), count)
    source_of, taker = mixed[0:count // 2 * 2:2], mixed[1:count // 2 * 2:2]
    margin = jnp.minimum(lengths[source_of] - 1, reach - lengths[taker]) // 2
    margin = jnp.where((source_of == order[0]) | (taker == order[0]) | (lengths[taker] == 0), 0, jnp.maximum(margin, 0))
    moved = jax.random.randint(jax.random.fold_in(own, 4), (count // 2,), 0, 1 << 20) % (margin + 1)
    lengths = lengths.at[source_of].add(-moved).at[taker].add(moved)
    labels = jnp.searchsorted(jnp.cumsum(lengths), jnp.arange(rows * top), side="right").astype(jnp.int32)
    listing = labels.reshape(top, rows).T
    listing = listing[jax.random.permutation(jax.random.fold_in(own, 1), rows)]
    turn = jax.random.randint(jax.random.fold_in(own, 2), (rows, 1), 0, top)
    return jnp.take_along_axis(listing, (jnp.arange(top)[None, :] + turn) % top, axis=1)


def portions_of(count, total, most, lean, full):
    loads = [(1 << 20) // math.isqrt(rank ** lean) + 1 for rank in range(1, count + 1)]
    largest = most if full else min(most, max(-(-total // count), total * loads[0] // sum(loads)))
    least = 1 if total - largest >= count - 1 else 0
    holding, rest = [largest] + [least] * (count - 1), total - largest - least * (count - 1)
    while rest > 0:
        movable = [i for i in range(1, count) if holding[i] < largest] or [i for i in range(1, count) if holding[i] < most]
        pool, remaining = sum([loads[i] for i in movable]), rest
        for i in movable:
            extra = min(most - holding[i], max(1, remaining * loads[i] // pool), rest)
            holding[i] = holding[i] + extra
            rest = rest - extra
    return np.array(holding)


def centred(stream_key, dims, scale, limit, cuts=(), kind=jnp.bfloat16):
    values = scale * jax.random.normal(stream_key, dims, jnp.float32)
    if cuts:
        values = values * steps_of(stream_key, dims, cuts, -0.22, 0.18)
    return jnp.clip(values, -limit, limit).astype(kind)


def setup_inputs(seed: int = 0, part: int = 0) -> dict:
    key_of = jax.random.split(jax.random.key(seed), 11)
    part_splits = jax.random.split(jax.random.fold_in(key_of[10], part), 11)
    resid = draw_resid(jax.random.fold_in(jax.random.fold_in(key_of[10], part), 71), part)
    queries = draw_queries(jax.random.fold_in(jax.random.fold_in(key_of[10], part), 71), part)
    keys = draw_keys(jax.random.fold_in(jax.random.fold_in(key_of[10], part), 71), part)
    values = centred(part_splits[3], (TOKENS, KV * HD), 1.0, 6.0, ((0, 8), (1, 2)))
    norm_gain = jnp.clip(1.0 + 0.18 * jax.random.normal(key_of[4], (D,), jnp.float32), 0.1, 1.9)
    expert_ids_keys = jax.random.split(jax.random.fold_in(part_splits[5], 1), TOKENS // TOK_DEV)
    expert_ids_turns = jax.random.permutation(jax.random.fold_in(part_splits[5], 3), TOKENS // TOK_DEV)
    expert_ids = jax.vmap(lambda own, number: deal_out(jax.random.fold_in(part_splits[5], 2), own, number, TOK_DEV, EXPERTS, TOPK, CAP, 2))(expert_ids_keys, expert_ids_turns).reshape((TOKENS, TOPK))
    gate_weights = jnp.clip(0.2 + 0.8 * jax.random.uniform(part_splits[6], (TOKENS, TOPK), jnp.float32) ** steps_of(part_splits[6], (TOKENS, TOPK), ((0, 8),), -0.2, 0.2), 0.2, 1.0)
    w_gate = centred(key_of[7], (2 * EXPERTS, D, FF // 2), D ** -0.5, 0.09375, ((0, 8), (2, 2)))
    w_up = centred(key_of[8], (2 * EXPERTS, D, FF // 2), D ** -0.5, 0.09375, ((0, 8), (2, 2)))
    w_down = centred(key_of[9], (2 * EXPERTS, FF // 2, D), FF ** -0.5, 0.15625, ((0, 8), (1, 2)))
    return {"resid": resid, "queries": queries, "keys": keys, "values": values, "norm_gain": norm_gain, "expert_ids": expert_ids, "gate_weights": gate_weights, "w_gate": w_gate, "w_up": w_up, "w_down": w_down}


def attend_all(queries, keys, values):
    group_size = HEADS // KV
    block_rows = min(TOKENS, 1024)
    score_scale = 1.0 / math.sqrt(HD)
    query_heads = queries.reshape(TOKENS, HEADS, HD)
    key_heads = keys.reshape(TOKENS, KV, HD)
    value_heads = values.reshape(TOKENS, KV, HD)

    def one_head(head_index):
        kv_index = head_index // group_size
        query_one = lax.dynamic_index_in_dim(query_heads, head_index, 1, keepdims=False)
        key_one = lax.dynamic_index_in_dim(key_heads, kv_index, 1, keepdims=False)
        value_one = lax.dynamic_index_in_dim(value_heads, kv_index, 1, keepdims=False)

        def one_block(query_block):
            scores = jnp.dot(query_block, key_one.T, preferred_element_type=jnp.float32) * score_scale
            row_max = lax.optimization_barrier(jnp.max(scores, axis=1, keepdims=True))
            raised = jnp.exp(scores - row_max)
            row_total = lax.optimization_barrier(jnp.sum(raised, axis=1, keepdims=True))
            mixed = jnp.dot(raised.astype(jnp.bfloat16), value_one, preferred_element_type=jnp.float32)
            return mixed / row_total
        blocks = query_one.reshape(TOKENS // block_rows, block_rows, HD)
        return lax.map(one_block, blocks).reshape(TOKENS, HD)
    gathered_heads = lax.map(one_head, jnp.arange(HEADS, dtype=jnp.int32))
    return jnp.transpose(gathered_heads, (1, 0, 2)).reshape(TOKENS, HEADS * HD).astype(jnp.bfloat16)

def experts_all(normed, expert_ids, gate_weights, w_gate, w_up, w_down):
    flat_ids = expert_ids.reshape(-1).astype(jnp.int32)
    sort_order = jnp.argsort(flat_ids, stable=True).astype(jnp.int32)
    sorted_ids = flat_ids[sort_order]
    expert_range = jnp.arange(EXPERTS, dtype=jnp.int32)
    starts = jnp.searchsorted(sorted_ids, expert_range).astype(jnp.int32)
    counts = lax.optimization_barrier(jnp.sum((flat_ids[:, None] == expert_range[None, :]).astype(jnp.int32), axis=0))
    slot_limit = N_DEV * CAP
    tokens_pad = jnp.concatenate([(sort_order // TOPK).astype(jnp.int32), jnp.zeros((slot_limit,), jnp.int32)])
    gates_pad = jnp.concatenate([gate_weights.reshape(-1)[sort_order], jnp.zeros((slot_limit,), jnp.float32)])
    quarter = FF // 4

    def one_expert(running, expert):
        start_at = starts[expert]
        rows_at = lax.dynamic_slice_in_dim(tokens_pad, start_at, slot_limit)
        weight = lax.dynamic_slice_in_dim(gates_pad, start_at, slot_limit)
        live = jnp.arange(slot_limit, dtype=jnp.int32) < counts[expert]
        weight = jnp.where(live, weight, 0.0)
        picked = normed[rows_at]
        result = jnp.zeros((slot_limit, D), jnp.float32)
        for half_index in range(2):
            shard = 2 * expert + half_index
            gate_shard = lax.dynamic_index_in_dim(w_gate, shard, 0, keepdims=False)
            up_shard = lax.dynamic_index_in_dim(w_up, shard, 0, keepdims=False)
            down_shard = lax.dynamic_index_in_dim(w_down, shard, 0, keepdims=False)
            for section in range(2):
                low = section * quarter
                gate_out = jnp.dot(picked, gate_shard[:, low:low + quarter], preferred_element_type=jnp.float32)
                up_out = jnp.dot(picked, up_shard[:, low:low + quarter], preferred_element_type=jnp.float32)
                activation = (jax.nn.silu(gate_out) * up_out).astype(jnp.bfloat16)
                partial_out = jnp.dot(activation, down_shard[low:low + quarter, :], preferred_element_type=jnp.float32).astype(jnp.bfloat16)
                result = result + partial_out.astype(jnp.float32)
        return (running.at[rows_at].add(result * weight[:, None]), None)
    moe_sum, _ = lax.scan(one_expert, jnp.zeros((TOKENS, D), jnp.float32), expert_range)
    return moe_sum

def reference(resid, queries, keys, values, norm_gain, expert_ids, gate_weights, w_gate, w_up, w_down):
    attended = attend_all(queries, keys, values)
    stream = resid.astype(jnp.float32) + attended.astype(jnp.float32)
    normed = (stream * lax.rsqrt(lax.optimization_barrier(jnp.mean(stream * stream, axis=-1, keepdims=True)) + 1e-06) * norm_gain).astype(jnp.bfloat16)
    moe_sum = experts_all(normed, expert_ids, gate_weights, w_gate, w_up, w_down)
    return (stream + moe_sum).astype(jnp.bfloat16)
```

```python
import functools
import math

import jax
import jax.numpy as jnp
from jax import lax
from jax.experimental import pallas as pl
from jax.experimental.pallas import tpu as pltpu
from jax.sharding import PartitionSpec as P

HD = 128
F32 = jnp.float32
BF16 = jnp.bfloat16
VMEM = pl.BlockSpec(memory_space=pltpu.VMEM)


def params(megabytes):
    return pltpu.CompilerParams(vmem_limit_bytes=megabytes * 1024 * 1024)


def cost(flops, moved):
    return pl.CostEstimate(flops=int(flops), bytes_accessed=int(moved), transcendentals=0)


def attend_kernel(blocks, kv_here, group_size, q_ref, resid_ref, *refs):
    kv_refs, (stream_ref, square_ref) = refs[:-2], refs[-2:]
    rows = q_ref.shape[0]
    factor = math.log2(math.e) / math.sqrt(HD)
    squares = jnp.zeros((rows, 1), F32)
    for g in range(kv_here):
        heads = [q_ref[:, (g * group_size + r) * HD : (g * group_size + r + 1) * HD] for r in range(group_size)]
        query = jnp.concatenate(heads, axis=0)
        run_max = None
        for block in blocks:
            keys = jnp.concatenate([kv_refs[i][:, g * HD : (g + 1) * HD] for i in block], axis=0)
            values = jnp.concatenate(
                [kv_refs[i][:, (kv_here + g) * HD : (kv_here + g + 1) * HD] for i in block], axis=0
            )
            scores = lax.dot_general(query, keys, (((1,), (1,)), ((), ())), preferred_element_type=F32)
            top = jnp.max(scores, axis=1, keepdims=True)
            new_max = top if run_max is None else jnp.maximum(run_max, top)
            raised = jnp.exp2((scores - new_max) * factor)
            total = jnp.sum(raised, axis=1, keepdims=True)
            mixed = jnp.dot(raised.astype(BF16), values, preferred_element_type=F32)
            if run_max is None:
                run_total, run_mixed = total, mixed
            else:
                old = jnp.exp2((run_max - new_max) * factor)
                run_total, run_mixed = run_total * old + total, run_mixed * old + mixed
            run_max = new_max
        attended = (run_mixed / run_total).astype(BF16).astype(F32)
        for r in range(group_size):
            low = (g * group_size + r) * HD
            stream = resid_ref[:, low : low + HD].astype(F32) + attended[r * rows : (r + 1) * rows]
            stream_ref[:, low : low + HD] = stream
            squares = squares + jnp.sum(stream * stream, axis=1, keepdims=True)
    square_ref[...] = jnp.broadcast_to(squares, square_ref.shape)


def attend_long(queries, resid_half, pieces):
    rows, kv_here = queries.shape[0], pieces[0].shape[1] // (2 * HD)
    grouped = queries.reshape(rows, kv_here, -1, HD)
    scale = 1.0 / math.sqrt(HD)
    state = None
    for i in range(0, len(pieces), 8):
        block = jnp.concatenate(pieces[i : i + 8], axis=0).reshape(-1, 2, kv_here, HD)
        scores = jnp.einsum("tgrd,ngd->grtn", grouped, block[:, 0], preferred_element_type=F32) * scale
        top = jnp.max(scores, axis=-1, keepdims=True)
        new_max = top if state is None else jnp.maximum(state[0], top)
        raised = jnp.exp(scores - new_max)
        total = jnp.sum(raised, axis=-1, keepdims=True)
        mixed = jnp.einsum("grtn,ngd->grtd", raised.astype(BF16), block[:, 1], preferred_element_type=F32)
        if state is not None:
            old = jnp.exp(state[0] - new_max)
            total, mixed = state[1] * old + total, state[2] * old + mixed
        state = (new_max, total, mixed)
    attended = (state[2] / state[1]).transpose(2, 0, 1, 3).reshape(rows, -1).astype(BF16)
    stream = resid_half.astype(F32) + attended.astype(F32)
    return stream, jnp.broadcast_to(jnp.sum(stream * stream, axis=1, keepdims=True), (rows, HD))


def pick_kernel(width, stream_ref, own_ref, other_ref, gain_ref, pick_ref, *outs):
    squares = own_ref[:, :1] + other_ref[:, :1]
    normed = (stream_ref[...] * lax.rsqrt(squares / width + 1e-06) * gain_ref[...]).astype(BF16)
    for k, out_ref in enumerate(outs):
        out_ref[...] = jnp.dot(pick_ref[k], normed, preferred_element_type=F32).astype(BF16)


def hidden_kernel(sec_ref, *refs):
    pieces, (gate_ref, up_ref, act_ref, gate_sum, up_sum) = refs[:8], refs[8:]
    step = pl.program_id(0)
    for j in range(4):

        @pl.when(step == j)
        def _(j=j):
            rows = jnp.concatenate([pieces[2 * j][...], pieces[2 * j + 1][...]], axis=0)
            gate = jnp.dot(rows, gate_ref[...], preferred_element_type=F32)
            up = jnp.dot(rows, up_ref[...], preferred_element_type=F32)
            if j == 0:
                gate_sum[...] = gate
                up_sum[...] = up
            elif j < 3:
                gate_sum[...] += gate
                up_sum[...] += up
            else:
                gate = gate_sum[...] + gate
                up = up_sum[...] + up
                act_ref[...] = (gate / (1.0 + jnp.exp(-gate)) * up).astype(BF16)


def down_kernel(own_act, other_act, own_w, other_w, keep_ref, send_ref):
    rows = keep_ref.shape[0]
    total = jnp.dot(own_act[...], own_w[...], preferred_element_type=F32)
    total = total + jnp.dot(other_act[...], other_w[...], preferred_element_type=F32)
    keep_ref[...] = total[:rows]
    send_ref[...] = total[rows:].astype(BF16)


def combine_kernel(stream_ref, high_ref, low_ref, *refs):
    returned, out_ref = refs[:-1], refs[-1]
    total = stream_ref[...]
    for k, ref in enumerate(returned):
        rows = ref[...]
        total = total + jnp.dot(high_ref[k], rows, preferred_element_type=F32)
        total = total + jnp.dot(low_ref[k], rows, preferred_element_type=F32)
    out_ref[...] = total.astype(BF16)


def body(resid, queries, keys, values, norm_gain, expert_ids, gate_weights, w_gate, w_up, w_down):
    rows, width = resid.shape
    half = width // 2
    quarter = half // 2
    heads_here = queries.shape[1] // HD
    kv_here = keys.shape[1] // HD
    group_size = heads_here // kv_here
    n_dev = lax.axis_size("dev")
    n_exp = n_dev // 2
    topk = expert_ids.shape[1]
    cap = max(2, (rows * topk * 5 + 4 * n_exp - 1) // (4 * n_exp))
    hidden = w_gate.shape[2]
    sec = lax.axis_index("sec")
    plane = lax.axis_index("dev") // 2

    def over_sec(a):
        return lax.ppermute(a, "sec", [(0, 1), (1, 0)])

    def over_y(a):
        return lax.ppermute(a, "dev", [(i, i ^ 1) for i in range(n_dev)])

    def over_z(a, k):
        return lax.ppermute(a, "dev", [(i, ((i // 2) ^ k) * 2 + i % 2) for i in range(n_dev)])

    own_kv = jnp.concatenate([keys, values], axis=1)
    kv_planes = [own_kv] + [over_z(own_kv, k) for k in range(1, n_exp)]
    pieces = kv_planes + [over_y(a) for a in kv_planes]
    down_own = lax.dynamic_slice_in_dim(w_down[0], sec * half, half, 1)
    down_other = over_sec(lax.dynamic_slice_in_dim(w_down[0], (1 - sec) * half, half, 1))

    experts = jnp.arange(n_exp, dtype=jnp.int32)
    onehot = (expert_ids[:, :, None] == experts[None, None, :]).astype(jnp.int32)
    onehot = onehot.reshape(rows * topk, n_exp)
    earlier = jnp.cumsum(onehot, axis=0) - onehot
    slot = jnp.sum(earlier * onehot, axis=1).reshape(rows, topk)
    target = (expert_ids ^ plane) * cap + slot
    placed = target[:, :, None] == jnp.arange(n_exp * cap, dtype=jnp.int32)[None, None, :]
    pick = jnp.sum(placed.astype(F32), axis=1).astype(BF16).T.reshape(n_exp, cap, rows)
    weight = jnp.sum(jnp.where(placed, gate_weights[:, :, None], 0.0), axis=1)
    weight = weight.reshape(rows, n_exp, cap).transpose(1, 0, 2)
    weight_high = weight.astype(BF16)
    weight_low = (weight - weight_high.astype(F32)).astype(BF16)

    resid_half = lax.dynamic_slice_in_dim(resid, sec * half, half, 1)
    gain_half = lax.dynamic_slice_in_dim(norm_gain, sec * half, half, 0).reshape(1, half)

    n_keys = rows * n_dev
    if n_dev <= 8:
        stream, squares = pl.pallas_call(
            functools.partial(attend_kernel, [list(range(len(pieces)))], kv_here, group_size),
            out_shape=(jax.ShapeDtypeStruct((rows, half), F32), jax.ShapeDtypeStruct((rows, HD), F32)),
            in_specs=[VMEM] * (2 + len(pieces)),
            out_specs=(VMEM, VMEM),
            compiler_params=params(56),
            cost_estimate=cost(4 * rows * half * n_keys, n_keys * kv_here * HD * 4 + rows * half * 8),
            name="attend",
        )(queries, resid_half, *pieces)
    else:
        stream, squares = attend_long(queries, resid_half, pieces)

    other_squares = over_sec(squares)
    sent = pl.pallas_call(
        functools.partial(pick_kernel, width),
        out_shape=[jax.ShapeDtypeStruct((cap, half), BF16)] * n_exp,
        in_specs=[VMEM] * 5,
        out_specs=[VMEM] * n_exp,
        compiler_params=params(32),
        cost_estimate=cost(2 * n_exp * cap * rows * half, rows * half * 4 + n_exp * cap * half * 2),
        name="pick",
    )(stream, squares, other_squares, gain_half, pick)

    def plane_gather(rows_here):
        first, second = rows_here[:, :quarter], rows_here[:, quarter:]
        first_x = over_sec(first)
        second_y = over_y(second)
        count = first.shape[0]
        first_y = over_y(jnp.stack([first, first_x]))
        second_x = over_sec(jnp.stack([second, second_y]))
        return [first, first_y[0], second, second_y, first_x, first_y[1], second_x[0], second_x[1]]

    def experts_of(parts):
        count = parts[0].shape[0]
        whole = [pl.BlockSpec((count, quarter), lambda j, s: (0, 0))] * 8
        weights = pl.BlockSpec((quarter, hidden), lambda j, s: ((j + 2 * s[0]) % 4, 0))
        act = pl.pallas_call(
            hidden_kernel,
            grid_spec=pltpu.PrefetchScalarGridSpec(
                num_scalar_prefetch=1,
                grid=(4,),
                in_specs=whole + [weights, weights],
                out_specs=pl.BlockSpec((2 * count, hidden), lambda j, s: (0, 0)),
                scratch_shapes=[pltpu.VMEM((2 * count, hidden), F32)] * 2,
            ),
            out_shape=jax.ShapeDtypeStruct((2 * count, hidden), BF16),
            compiler_params=params(32),
            cost_estimate=cost(8 * count * width * hidden, 4 * width * hidden),
            name="hidden",
        )(sec.astype(jnp.int32).reshape(1), *parts, w_gate[0], w_up[0])
        other_act = over_sec(act)
        keep, send = pl.pallas_call(
            down_kernel,
            out_shape=(jax.ShapeDtypeStruct((count, half), F32), jax.ShapeDtypeStruct((count, half), BF16)),
            in_specs=[VMEM] * 4,
            out_specs=(VMEM, VMEM),
            compiler_params=params(32),
            cost_estimate=cost(8 * count * half * hidden, 4 * half * hidden),
            name="down",
        )(act, other_act, down_own, down_other)
        return (keep + over_y(send).astype(F32)).astype(BF16)

    arrived = [sent[0]] + [over_z(sent[k], k) for k in range(1, n_exp)]
    n_groups = min(4, n_exp)
    each = n_exp // n_groups
    returned = [None] * n_exp
    for g in range(n_groups):
        members = list(range(g * each, (g + 1) * each))
        block = arrived[members[0]] if each == 1 else jnp.concatenate([arrived[k] for k in members], axis=0)
        result = experts_of(plane_gather(block))
        for n, k in enumerate(members):
            part = result if each == 1 else result[n * cap : (n + 1) * cap]
            returned[k] = part if k == 0 else over_z(part, k)

    return pl.pallas_call(
        combine_kernel,
        out_shape=jax.ShapeDtypeStruct((rows, half), BF16),
        in_specs=[VMEM] * (3 + n_exp),
        out_specs=VMEM,
        compiler_params=params(32),
        cost_estimate=cost(4 * n_exp * cap * rows * half, rows * half * 6 + n_exp * cap * half * 2),
        name="combine",
    )(stream, weight_high, weight_low, *returned)


def solution(mesh):
    in_specs = (
        P(("rep", "dev"), None),
        P(("rep", "dev"), "sec"),
        P(("rep", "dev"), "sec"),
        P(("rep", "dev"), "sec"),
        P(),
        P(("rep", "dev"), None),
        P(("rep", "dev"), None),
        P("dev", None, "sec"),
        P("dev", None, "sec"),
        P("dev", "sec", None),
    )
    out_specs = P(("rep", "dev"), "sec")
    return jax.shard_map(body, mesh=mesh, in_specs=in_specs, out_specs=out_specs, check_vma=False)
```

```python
import functools
import math

import jax
import jax.numpy as jnp
from jax import lax
from jax.experimental import pallas as pl
from jax.experimental.pallas import tpu as pltpu
from jax.sharding import PartitionSpec as P

HD = 128
F32 = jnp.float32
BF16 = jnp.bfloat16
VMEM = pl.BlockSpec(memory_space=pltpu.VMEM)
ANY = pl.BlockSpec(memory_space=pl.ANY)


def params():
    return pltpu.CompilerParams(vmem_limit_bytes=20 * 1024 * 1024)


def cost(flops, moved):
    return pl.CostEstimate(flops=int(flops), bytes_accessed=int(moved), transcendentals=0)


def pack_kernel(keys_ref, values_ref, out_ref):
    size = keys_ref.shape[1]
    out_ref[:, :size] = keys_ref[...]
    out_ref[:, size:] = values_ref[...]


def stage_kernel(sec_ref, q_ref, resid_ref, gain_ref, q_out, resid_out, gain_out, inverse_out):
    half = q_out.shape[1]
    q_out[...] = q_ref[...]
    low = pl.multiple_of(sec_ref[0] * half, half)
    resid_out[...] = resid_ref[:, pl.ds(low, half)]
    gain_out[...] = gain_ref[:, pl.ds(low, half)]
    inverse_out[:, :half] = 1.0 / gain_ref[:, pl.ds(low, half)]
    inverse_out[:, half:] = 1.0 / gain_ref[:, pl.ds(pl.multiple_of(half - low, half), half)]


def weights_kernel(sec_ref, gate_ref, up_ref, out_ref, sems):
    half, hidden = gate_ref.shape[0] // 2, gate_ref.shape[1]
    copies = []
    for c in range(2):
        low = pl.multiple_of(lax.rem(sec_ref[0] + c, 2) * half, half)
        for n, ref in enumerate((gate_ref, up_ref)):
            target = out_ref.at[c * half : (c + 1) * half, n * hidden : (n + 1) * hidden]
            copies.append(pltpu.make_async_copy(ref.at[pl.ds(low, half)], target, sems.at[2 * c + n]))
            copies[-1].start()
    for copy in copies:
        copy.wait()


def attend_kernel(n_pieces, q_ref, resid_ref, gain_ref, pick_ref, *refs):
    kv_refs, stream_ref, outs = refs[:n_pieces], refs[n_pieces], refs[n_pieces + 1 :]
    rows = q_ref.shape[0]
    kv_here = kv_refs[0].shape[1] // (2 * HD)
    group_size = q_ref.shape[1] // HD // kv_here
    factor = math.log2(math.e) / math.sqrt(HD)
    for g in range(kv_here):
        heads = [q_ref[:, (g * group_size + r) * HD : (g * group_size + r + 1) * HD] for r in range(group_size)]
        query = jnp.concatenate(heads, axis=0)
        keys = jnp.concatenate([ref[:, g * HD : (g + 1) * HD] for ref in kv_refs], axis=0)
        values = jnp.concatenate([ref[:, (kv_here + g) * HD : (kv_here + g + 1) * HD] for ref in kv_refs], axis=0)
        scores = lax.dot_general(query, keys, (((1,), (1,)), ((), ())), preferred_element_type=F32)
        raised = jnp.exp2((scores - jnp.max(scores, axis=1, keepdims=True)) * factor)
        total = jnp.sum(raised, axis=1, keepdims=True)
        mixed = jnp.dot(raised.astype(BF16), values, preferred_element_type=F32)
        attended = (mixed / total).astype(BF16).astype(F32)
        for r in range(group_size):
            low = (g * group_size + r) * HD
            stream_ref[:, low : low + HD] = resid_ref[:, low : low + HD].astype(F32) + attended[r * rows : (r + 1) * rows]
    scaled = (stream_ref[...] * gain_ref[...]).astype(BF16)
    for k, out_ref in enumerate(outs):
        out_ref[...] = jnp.dot(pick_ref[k], scaled, preferred_element_type=F32).astype(BF16)


def attend_long(queries, resid, gain, pick, pieces):
    rows, kv_here = queries.shape[0], pieces[0].shape[1] // (2 * HD)
    grouped = queries.reshape(rows, kv_here, -1, HD)
    scale = 1.0 / math.sqrt(HD)
    state = None
    for i in range(0, len(pieces), 8):
        block = jnp.concatenate(pieces[i : i + 8], axis=0).reshape(-1, 2, kv_here, HD)
        scores = jnp.einsum("tgrd,ngd->grtn", grouped, block[:, 0], preferred_element_type=F32) * scale
        top = jnp.max(scores, axis=-1, keepdims=True)
        new_max = top if state is None else jnp.maximum(state[0], top)
        raised = jnp.exp(scores - new_max)
        total = jnp.sum(raised, axis=-1, keepdims=True)
        mixed = jnp.einsum("grtn,ngd->grtd", raised.astype(BF16), block[:, 1], preferred_element_type=F32)
        if state is not None:
            old = jnp.exp(state[0] - new_max)
            total, mixed = state[1] * old + total, state[2] * old + mixed
        state = (new_max, total, mixed)
    attended = (state[2] / state[1]).transpose(2, 0, 1, 3).reshape(rows, -1).astype(BF16)
    stream = resid.astype(F32) + attended.astype(F32)
    scaled = (stream * gain).astype(BF16)
    return [stream] + [jnp.dot(p, scaled, preferred_element_type=F32).astype(BF16) for p in pick]


def down_weights_kernel(index_ref, own_ref, near_ref, far_ref, out_ref, sems):
    hidden, quarter = near_ref.shape
    low = pl.multiple_of(index_ref[0] * 2 * quarter, quarter)
    near = pl.multiple_of(index_ref[1] * quarter, quarter)
    other = pl.multiple_of((1 - index_ref[1]) * quarter, quarter)
    copies = [
        pltpu.make_async_copy(own_ref.at[:, pl.ds(low, 2 * quarter)], out_ref.at[:hidden, :], sems.at[0]),
        pltpu.make_async_copy(near_ref, out_ref.at[hidden:, pl.ds(near, quarter)], sems.at[1]),
        pltpu.make_async_copy(far_ref, out_ref.at[hidden:, pl.ds(other, quarter)], sems.at[2]),
    ]
    for copy in copies:
        copy.start()
    for copy in copies:
        copy.wait()


def hidden_kernel(width, own_ref, y_ref, x_ref, both_ref, weights_ref, inverse_ref, act_ref):
    half, hidden = own_ref.shape[1], act_ref.shape[1]
    total = square = 0.0
    for c, refs in enumerate(((own_ref, y_ref), (x_ref, both_ref))):
        rows = jnp.concatenate([ref[...] for ref in refs], axis=0)
        columns = slice(c * half, (c + 1) * half)
        total = total + jnp.dot(rows, weights_ref[columns, :], preferred_element_type=F32)
        stream = rows.astype(F32) * inverse_ref[:, columns]
        square = square + jnp.sum(stream * stream, axis=1, keepdims=True)
    total = total * lax.rsqrt(square / width + 1e-06)
    gate, up = total[:, :hidden], total[:, hidden:]
    act_ref[...] = (gate / (1.0 + jnp.exp(-gate)) * up).astype(BF16)


def down_kernel(own_act, other_act, w_ref, keep_ref, send_ref):
    rows = keep_ref.shape[0]
    act = jnp.concatenate([own_act[...], other_act[...]], axis=1)
    total = jnp.dot(act, w_ref[...], preferred_element_type=F32)
    keep_ref[...] = total[:rows]
    send_ref[...] = total[rows:].astype(BF16)


def combine_kernel(stream_ref, high_ref, low_ref, *refs):
    returned, out_ref = refs[:-1], refs[-1]
    total = stream_ref[...]
    for k, ref in enumerate(returned):
        rows = ref[...]
        total = total + jnp.dot(high_ref[k], rows, preferred_element_type=F32)
        total = total + jnp.dot(low_ref[k], rows, preferred_element_type=F32)
    out_ref[...] = total.astype(BF16)


def near(values):
    return [pltpu.with_memory_space_constraint(v, pltpu.VMEM) for v in values]


def far(values):
    return [pltpu.with_memory_space_constraint(v, pltpu.HBM) for v in values]


def after(value, *others):
    return lax.optimization_barrier((value, *others))[0]


def body(resid, queries, keys, values, norm_gain, expert_ids, gate_weights, w_gate, w_up, w_down):
    rows, width = resid.shape
    half = width // 2
    quarter = half // 2
    n_dev = lax.axis_size("dev")
    n_exp = n_dev // 2
    topk = expert_ids.shape[1]
    cap = max(2, (rows * topk * 5 + 4 * n_exp - 1) // (4 * n_exp))
    hidden = w_gate.shape[2]
    sec = lax.axis_index("sec").astype(jnp.int32)
    rep = lax.axis_index("rep").astype(jnp.int32)
    plane = lax.axis_index("dev").astype(jnp.int32) // 2

    def over_sec(a):
        return lax.ppermute(a, "sec", [(0, 1), (1, 0)])

    def over_rep(a):
        return lax.ppermute(a, "rep", [(0, 1), (1, 0)])

    def over_y(a):
        return lax.ppermute(a, "dev", [(i, i ^ 1) for i in range(n_dev)])

    def over_z(a, k):
        return lax.ppermute(a, "dev", [(i, ((i // 2) ^ k) * 2 + i % 2) for i in range(n_dev)])

    own_kv = pl.pallas_call(
        pack_kernel,
        out_shape=jax.ShapeDtypeStruct((rows, 2 * keys.shape[1]), BF16),
        in_specs=[VMEM] * 2,
        out_specs=VMEM,
        compiler_params=params(),
        cost_estimate=cost(0, 4 * keys.size * 2),
        name="pack",
    )(keys, values)
    planes = [own_kv] + [over_z(own_kv, k) for k in range(1, n_exp)]
    pieces = planes + [over_y(a) for a in planes]

    part = lax.dynamic_slice_in_dim(w_down[0], ((1 - sec) * 2 + rep) * quarter, quarter, 1)
    down_near = over_sec(part)
    down_far = over_rep(after(down_near, pieces[n_exp + 1]))

    experts = jnp.arange(n_exp, dtype=jnp.int32)
    onehot = (expert_ids[:, :, None] == experts[None, None, :]).astype(jnp.int32)
    onehot = onehot.reshape(rows * topk, n_exp)
    earlier = jnp.cumsum(onehot, axis=0) - onehot
    slot = jnp.sum(earlier * onehot, axis=1).reshape(rows, topk)
    target = (expert_ids ^ plane) * cap + slot
    placed = target[:, :, None] == jnp.arange(n_exp * cap, dtype=jnp.int32)[None, None, :]
    pick = jnp.sum(placed.astype(F32), axis=1).astype(BF16).T.reshape(n_exp, cap, rows)
    weight = jnp.sum(jnp.where(placed, gate_weights[:, :, None], 0.0), axis=1)
    weight = weight.reshape(rows, n_exp, cap).transpose(1, 0, 2)
    weight_high = weight.astype(BF16)
    weight_low = (weight - weight_high.astype(F32)).astype(BF16)
    gain = norm_gain.reshape(1, width)
    index = jnp.stack([sec, rep])
    smem = pl.BlockSpec(memory_space=pltpu.SMEM)
    staged = pl.pallas_call(
        stage_kernel,
        out_shape=[
            pltpu.VMEM((rows, half), BF16),
            pltpu.VMEM((rows, half), BF16),
            pltpu.VMEM((1, half), F32),
            pltpu.VMEM((1, width), F32),
        ],
        in_specs=[smem] + [VMEM] * 3,
        out_specs=[VMEM] * 4,
        compiler_params=params(),
        name="stage",
    )(sec.reshape(1), *far([queries, resid, gain]))
    weights = pl.pallas_call(
        weights_kernel,
        out_shape=pltpu.VMEM((width, 2 * hidden), BF16),
        in_specs=[smem] + [ANY] * 2,
        out_specs=VMEM,
        scratch_shapes=[pltpu.SemaphoreType.DMA((4,))],
        compiler_params=params(),
        name="weights",
    )(sec.reshape(1), *far([w_gate[0], w_up[0]]))
    tied = lax.optimization_barrier((pieces[1], pick, weight_high, weight_low, index, weights, down_far, *staged))
    pieces[1], pick, weight_high, weight_low, index, weights, down_far, *staged = tied
    queries, resid, gain, inverse = staged

    if n_dev > 8:
        stream, *sent = attend_long(queries, resid, gain, pick, pieces)
    else:
        n_keys = rows * n_dev
        stream, *sent = pl.pallas_call(
            functools.partial(attend_kernel, len(pieces)),
            in_specs=[VMEM] * (4 + len(pieces)),
            out_specs=[VMEM] * (1 + n_exp),
            out_shape=[pltpu.HBM((rows, half), F32)] + [jax.ShapeDtypeStruct((cap, half), BF16)] * n_exp,
            compiler_params=params(),
            cost_estimate=cost(4 * rows * half * n_keys, n_keys * half * 2),
            name="attend",
        )(queries, resid, gain, pick, *pieces)

    arrived = [sent[0]] + [over_z(sent[k], k) for k in range(1, n_exp)]
    down_weights = pl.pallas_call(
        down_weights_kernel,
        out_shape=pltpu.VMEM((2 * hidden, half), BF16),
        in_specs=[smem] + [ANY] * 3,
        out_specs=VMEM,
        scratch_shapes=[pltpu.SemaphoreType.DMA((3,))],
        compiler_params=params(),
        name="down_weights",
    )(after(index, stream), *far([w_down[0], down_near, down_far]))
    arrived[0], down_weights = lax.optimization_barrier((arrived[0], down_weights))
    each = max(1, n_exp // 4)
    if each > 1:
        arrived = [jnp.concatenate(arrived[i : i + each], axis=0) for i in range(0, n_exp, each)]

    def plane_gather(number, own):
        if number % 2 == 0:
            from_x, from_y = over_sec(own), over_y(own)
            return own, from_y, from_x, over_y(from_x)
        from_y, from_x = over_y(own), over_sec(own)
        return own, from_y, from_x, over_sec(from_y)

    def experts_of(gathered):
        count = gathered[0].shape[0]
        act = pl.pallas_call(
            functools.partial(hidden_kernel, width),
            in_specs=[VMEM] * 6,
            out_specs=VMEM,
            out_shape=jax.ShapeDtypeStruct((2 * count, hidden), BF16),
            compiler_params=params(),
            cost_estimate=cost(8 * count * width * hidden, 4 * width * hidden),
            name="hidden",
        )(*gathered, weights, inverse)
        keep, send = pl.pallas_call(
            down_kernel,
            in_specs=[VMEM] * 3,
            out_specs=[VMEM] * 2,
            out_shape=[jax.ShapeDtypeStruct((count, half), F32), jax.ShapeDtypeStruct((count, half), BF16)],
            compiler_params=params(),
            cost_estimate=cost(8 * count * half * hidden, 4 * half * hidden),
            name="down",
        )(act, over_sec(act), down_weights)
        return (keep + over_y(send).astype(F32)).astype(BF16)

    returned = [None] * n_exp
    gathered = []
    for g, block in enumerate(arrived):
        if g > 0:
            block = after(block, *gathered[-1][1:3])
        gathered.append(plane_gather(g, block))
    for g in range(len(arrived)):
        result = experts_of(gathered[g])
        for n, k in enumerate(range(g * each, (g + 1) * each)):
            back = result if each == 1 else result[n * cap : (n + 1) * cap]
            returned[k] = back if k == 0 else over_z(back, k)

    return pl.pallas_call(
        combine_kernel,
        out_shape=jax.ShapeDtypeStruct((rows, half), BF16),
        in_specs=[VMEM] * (3 + n_exp),
        out_specs=VMEM,
        compiler_params=params(),
        cost_estimate=cost(4 * n_exp * cap * rows * half, rows * half * 6 + n_exp * cap * half * 2),
        name="combine",
    )(stream, weight_high, weight_low, *returned)


def solution(mesh):
    in_specs = (
        P(("rep", "dev"), None),
        P(("rep", "dev"), "sec"),
        P(("rep", "dev"), "sec"),
        P(("rep", "dev"), "sec"),
        P(),
        P(("rep", "dev"), None),
        P(("rep", "dev"), None),
        P("dev", None, "sec"),
        P("dev", None, "sec"),
        P("dev", "sec", None),
    )
    out_specs = P(("rep", "dev"), "sec")
    return jax.shard_map(body, mesh=mesh, in_specs=in_specs, out_specs=out_specs, check_vma=False)
```

```python
import functools
import math

import jax
import jax.numpy as jnp
from jax import lax
from jax.experimental import pallas as pl
from jax.experimental.pallas import tpu as pltpu
from jax.sharding import PartitionSpec as P

HD = 128
F32 = jnp.float32
BF16 = jnp.bfloat16
VMEM = pl.BlockSpec(memory_space=pltpu.VMEM)
ANY = pl.BlockSpec(memory_space=pl.ANY)


def params():
    return pltpu.CompilerParams(vmem_limit_bytes=28 * 1024 * 1024)


def cost(flops, moved):
    return pl.CostEstimate(flops=int(flops), bytes_accessed=int(moved), transcendentals=0)


def copy_all(pairs, sems):
    copies = [pltpu.make_async_copy(source, target, sems.at[i]) for i, (source, target) in enumerate(pairs)]
    for copy in copies:
        copy.start()
    for copy in copies:
        copy.wait()


def pack_kernel(keys_ref, values_ref, kv_out, sems):
    size = keys_ref.shape[1]
    copy_all([(keys_ref, kv_out.at[:, :size]), (values_ref, kv_out.at[:, size:])], sems)


def stage_kernel(sec_ref, q_ref, resid_ref, gain_ref, gate_ref, up_ref, down_ref, *refs):
    q_out, resid_out, gain_out, columns_out, down_out, sems = refs
    half, hidden = q_out.shape[1], gate_ref.shape[1]
    low = pl.multiple_of(sec_ref[0] * half, half)
    rest = pl.multiple_of((1 - sec_ref[0]) * half, half)
    pairs = [
        (q_ref, q_out),
        (resid_ref.at[:, pl.ds(low, half)], resid_out),
        (gain_ref.at[:, pl.ds(low, half)], gain_out.at[:, :half]),
        (gain_ref.at[:, pl.ds(rest, half)], gain_out.at[:, half:]),
        (down_ref.at[:, pl.ds(low, half)], down_out),
    ]
    for c, start in enumerate((low, rest)):
        for n, ref in enumerate((gate_ref, up_ref)):
            target = columns_out.at[c * half : (c + 1) * half, n * hidden : (n + 1) * hidden]
            pairs.append((ref.at[pl.ds(start, half)], target))
    copy_all(pairs, sems)


def attend_kernel(n_pieces, q_ref, resid_ref, gain_ref, pick_ref, *refs):
    kv_refs, stream_ref, outs = refs[:n_pieces], refs[n_pieces], refs[n_pieces + 1 :]
    rows = q_ref.shape[0]
    kv_here = kv_refs[0].shape[1] // (2 * HD)
    group_size = q_ref.shape[1] // HD // kv_here
    factor = math.log2(math.e) / math.sqrt(HD)
    for g in range(kv_here):
        heads = [q_ref[:, (g * group_size + r) * HD : (g * group_size + r + 1) * HD] for r in range(group_size)]
        query = jnp.concatenate(heads, axis=0)
        keys = jnp.concatenate([ref[:, g * HD : (g + 1) * HD] for ref in kv_refs], axis=0)
        values = jnp.concatenate([ref[:, (kv_here + g) * HD : (kv_here + g + 1) * HD] for ref in kv_refs], axis=0)
        scores = lax.dot_general(query, keys, (((1,), (1,)), ((), ())), preferred_element_type=F32)
        raised = jnp.exp2((scores - jnp.max(scores, axis=1, keepdims=True)) * factor)
        total = jnp.sum(raised, axis=1, keepdims=True)
        mixed = jnp.dot(raised.astype(BF16), values, preferred_element_type=F32)
        attended = (mixed / total).astype(BF16).astype(F32)
        for r in range(group_size):
            low = (g * group_size + r) * HD
            stream_ref[:, low : low + HD] = resid_ref[:, low : low + HD].astype(F32) + attended[r * rows : (r + 1) * rows]
    scaled = (stream_ref[...] * gain_ref[:, : q_ref.shape[1]]).astype(BF16)
    for k, out_ref in enumerate(outs):
        out_ref[...] = jnp.dot(pick_ref[k], scaled, preferred_element_type=F32).astype(BF16)


def attend_long(queries, resid, gain, pick, pieces):
    rows, kv_here = queries.shape[0], pieces[0].shape[1] // (2 * HD)
    grouped = queries.reshape(rows, kv_here, -1, HD)
    scale = 1.0 / math.sqrt(HD)
    state = None
    for i in range(0, len(pieces), 8):
        block = jnp.concatenate(pieces[i : i + 8], axis=0).reshape(-1, 2, kv_here, HD)
        scores = jnp.einsum("tgrd,ngd->grtn", grouped, block[:, 0], preferred_element_type=F32) * scale
        top = jnp.max(scores, axis=-1, keepdims=True)
        new_max = top if state is None else jnp.maximum(state[0], top)
        raised = jnp.exp(scores - new_max)
        total = jnp.sum(raised, axis=-1, keepdims=True)
        mixed = jnp.einsum("grtn,ngd->grtd", raised.astype(BF16), block[:, 1], preferred_element_type=F32)
        if state is not None:
            old = jnp.exp(state[0] - new_max)
            total, mixed = state[1] * old + total, state[2] * old + mixed
        state = (new_max, total, mixed)
    attended = (state[2] / state[1]).transpose(2, 0, 1, 3).reshape(rows, -1).astype(BF16)
    stream = resid.astype(F32) + attended.astype(F32)
    scaled = (stream * gain[:, : queries.shape[1]]).astype(BF16)
    return [stream] + [jnp.dot(p, scaled, preferred_element_type=F32).astype(BF16) for p in pick]


def hidden_kernel(width, own_ref, y_ref, x_ref, both_ref, weights_ref, gain_ref, act_ref):
    half, hidden = own_ref.shape[1], act_ref.shape[1]
    total = square = 0.0
    for c, refs in enumerate(((own_ref, y_ref), (x_ref, both_ref))):
        rows = jnp.concatenate([ref[...] for ref in refs], axis=0)
        columns = slice(c * half, (c + 1) * half)
        total = total + jnp.dot(rows, weights_ref[columns, :], preferred_element_type=F32)
        stream = rows.astype(F32) * (1.0 / gain_ref[:, columns])
        square = square + jnp.sum(stream * stream, axis=1, keepdims=True)
    total = total * lax.rsqrt(square / width + 1e-06)
    gate, up = total[:, :hidden], total[:, hidden:]
    act_ref[...] = (gate / (1.0 + jnp.exp(-gate)) * up).astype(BF16)


def down_kernel(rep_ref, own_act, other_act, own_ref, near_ref, far_ref, keep_ref, send_ref, total_ref):
    rows, quarter = keep_ref.shape[0], near_ref.shape[1]
    total_ref[...] = jnp.dot(own_act[...], own_ref[...], preferred_element_type=F32)
    for place, ref in ((rep_ref[0], near_ref), (1 - rep_ref[0], far_ref)):
        columns = pl.ds(pl.multiple_of(place * quarter, quarter), quarter)
        total_ref[:, columns] += jnp.dot(other_act[...], ref[...], preferred_element_type=F32)
    keep_ref[...] = total_ref[:rows]
    send_ref[...] = total_ref[rows:].astype(BF16)


def combine_kernel(stream_ref, high_ref, low_ref, *refs):
    returned, out_ref = refs[:-1], refs[-1]
    total = stream_ref[...]
    for k, ref in enumerate(returned):
        rows = ref[...]
        total = total + jnp.dot(high_ref[k], rows, preferred_element_type=F32)
        total = total + jnp.dot(low_ref[k], rows, preferred_element_type=F32)
    out_ref[...] = total.astype(BF16)


def near(values):
    return [pltpu.with_memory_space_constraint(v, pltpu.VMEM) for v in values]


def far(values):
    return [pltpu.with_memory_space_constraint(v, pltpu.HBM) for v in values]


def after(value, *others):
    return lax.optimization_barrier((value, *others))[0]


def body(resid, queries, keys, values, norm_gain, expert_ids, gate_weights, w_gate, w_up, w_down):
    rows, width = resid.shape
    half = width // 2
    quarter = half // 2
    n_dev = lax.axis_size("dev")
    n_exp = n_dev // 2
    topk = expert_ids.shape[1]
    cap = max(2, (rows * topk * 5 + 4 * n_exp - 1) // (4 * n_exp))
    hidden = w_gate.shape[2]
    sec = lax.axis_index("sec").astype(jnp.int32)
    rep = lax.axis_index("rep").astype(jnp.int32)
    plane = lax.axis_index("dev").astype(jnp.int32) // 2

    def over_sec(a):
        return lax.ppermute(a, "sec", [(0, 1), (1, 0)])

    def over_rep(a):
        return lax.ppermute(a, "rep", [(0, 1), (1, 0)])

    def over_y(a):
        return lax.ppermute(a, "dev", [(i, i ^ 1) for i in range(n_dev)])

    def over_z(a, k):
        return lax.ppermute(a, "dev", [(i, ((i // 2) ^ k) * 2 + i % 2) for i in range(n_dev)])

    own_kv = pl.pallas_call(
        pack_kernel,
        out_shape=jax.ShapeDtypeStruct((rows, 2 * keys.shape[1]), BF16),
        in_specs=[ANY] * 2,
        out_specs=VMEM,
        scratch_shapes=[pltpu.SemaphoreType.DMA((2,))],
        compiler_params=params(),
        name="pack",
    )(*far([keys, values]))
    planes = [own_kv] + [over_z(own_kv, k) for k in range(1, n_exp)]
    pieces = planes + [over_y(a) for a in planes]

    part = lax.dynamic_slice_in_dim(w_down[0], ((1 - sec) * 2 + rep) * quarter, quarter, 1)
    down_near = over_sec(after(part, planes[1]))

    experts = jnp.arange(n_exp, dtype=jnp.int32)
    onehot = (expert_ids[:, :, None] == experts[None, None, :]).astype(jnp.int32)
    onehot = onehot.reshape(rows * topk, n_exp)
    earlier = jnp.cumsum(onehot, axis=0) - onehot
    slot = jnp.sum(earlier * onehot, axis=1).reshape(rows, topk)
    target = (expert_ids ^ plane) * cap + slot
    placed = target[:, :, None] == jnp.arange(n_exp * cap, dtype=jnp.int32)[None, None, :]
    pick = jnp.sum(placed.astype(F32), axis=1).astype(BF16).T.reshape(n_exp, cap, rows)
    weight = jnp.sum(jnp.where(placed, gate_weights[:, :, None], 0.0), axis=1)
    weight = weight.reshape(rows, n_exp, cap).transpose(1, 0, 2)
    weight_high = weight.astype(BF16)
    weight_low = (weight - weight_high.astype(F32)).astype(BF16)
    smem = pl.BlockSpec(memory_space=pltpu.SMEM)
    staged = pl.pallas_call(
        stage_kernel,
        out_shape=[
            pltpu.VMEM((rows, half), BF16),
            pltpu.VMEM((rows, half), BF16),
            pltpu.VMEM((1, width), F32),
            pltpu.VMEM((width, 2 * hidden), BF16),
            pltpu.VMEM((hidden, half), BF16),
        ],
        in_specs=[smem] + [ANY] * 6,
        out_specs=[VMEM] * 5,
        scratch_shapes=[pltpu.SemaphoreType.DMA((9,))],
        compiler_params=params(),
        name="stage",
    )(sec.reshape(1), *far([queries, resid, norm_gain.reshape(1, width), w_gate[0], w_up[0], w_down[0]]))
    tied = lax.optimization_barrier((pieces[1], pick, weight_high, weight_low, *staged))
    pieces[1], pick, weight_high, weight_low, *staged = tied
    queries, resid, gain, columns, down_own = staged

    if n_dev > 8:
        stream, *sent = attend_long(queries, resid, gain, pick, pieces)
    else:
        n_keys = rows * n_dev
        stream, *sent = pl.pallas_call(
            functools.partial(attend_kernel, len(pieces)),
            in_specs=[VMEM] * (4 + len(pieces)),
            out_specs=[VMEM] * (1 + n_exp),
            out_shape=[pltpu.HBM((rows, half), F32)] + [jax.ShapeDtypeStruct((cap, half), BF16)] * n_exp,
            compiler_params=params(),
            cost_estimate=cost(4 * rows * half * n_keys, n_keys * half * 2),
            name="attend",
        )(queries, resid, gain, pick, *pieces)

    arrived = [sent[0]] + [None] * (n_exp - 1)
    for k in range(1, n_exp):
        arrived[k] = over_z(after(sent[k], arrived[1]) if k == 3 else sent[k], k)
    down_far = over_rep(after(down_near, stream))
    arrived[1] = after(arrived[1], down_far)
    each = max(1, n_exp // 4)
    if each > 1:
        arrived = [jnp.concatenate(arrived[i : i + each], axis=0) for i in range(0, n_exp, each)]

    def plane_gather(number, own):
        if number < 2:
            from_x, from_y = over_sec(own), over_y(own)
            return own, from_y, from_x, over_y(from_x)
        from_y, from_x = over_y(own), over_sec(own)
        return own, from_y, from_x, over_sec(from_y)

    def hidden_of(gathered):
        count = gathered[0].shape[0]
        return pl.pallas_call(
            functools.partial(hidden_kernel, width),
            in_specs=[VMEM] * 6,
            out_specs=VMEM,
            out_shape=jax.ShapeDtypeStruct((2 * count, hidden), BF16),
            compiler_params=params(),
            cost_estimate=cost(8 * count * width * hidden, 4 * width * hidden),
            name="hidden",
        )(*gathered, columns, gain)

    def down_of(act, other_act):
        count = act.shape[0] // 2
        return pl.pallas_call(
            down_kernel,
            in_specs=[smem] + [VMEM] * 5,
            out_specs=[VMEM] * 2,
            out_shape=[jax.ShapeDtypeStruct((count, half), F32), jax.ShapeDtypeStruct((count, half), BF16)],
            scratch_shapes=[pltpu.VMEM((2 * count, half), F32)],
            compiler_params=params(),
            cost_estimate=cost(8 * count * half * hidden, 4 * half * hidden),
            name="down",
        )(rep.reshape(1), act, other_act, down_own, down_near, down_far)

    acts, sends, results, returned = [], [], [], [None] * n_exp
    gathered = [plane_gather(g, block) for g, block in enumerate(arrived)]
    for g, (own, *others) in enumerate(gathered):
        if g > 1:
            own = after(own, sends[g - 2])
        acts.append(hidden_of((own, *others)))
        other_act = over_sec(acts[g])
        if g > 1:
            other_act = after(other_act, results[g - 2])
        keep, send = down_of(acts[g], other_act)
        sends.append(send)
        results.append((keep + over_y(send).astype(F32)).astype(BF16))
        for n, k in enumerate(range(g * each, (g + 1) * each)):
            back = results[g] if each == 1 else results[g][n * cap : (n + 1) * cap]
            returned[k] = back if k == 0 else over_z(back, k)

    return pl.pallas_call(
        combine_kernel,
        out_shape=jax.ShapeDtypeStruct((rows, half), BF16),
        in_specs=[VMEM] * (3 + n_exp),
        out_specs=VMEM,
        compiler_params=params(),
        cost_estimate=cost(4 * n_exp * cap * rows * half, rows * half * 6 + n_exp * cap * half * 2),
        name="combine",
    )(stream, weight_high, weight_low, *returned)


def solution(mesh):
    in_specs = (
        P(("rep", "dev"), None),
        P(("rep", "dev"), "sec"),
        P(("rep", "dev"), "sec"),
        P(("rep", "dev"), "sec"),
        P(),
        P(("rep", "dev"), None),
        P(("rep", "dev"), None),
        P("dev", None, "sec"),
        P("dev", None, "sec"),
        P("dev", "sec", None),
    )
    out_specs = P(("rep", "dev"), "sec")
    return jax.shard_map(body, mesh=mesh, in_specs=in_specs, out_specs=out_specs, check_vma=False)
```

```python
import functools
import math

import jax
import jax.numpy as jnp
from jax import lax
from jax.experimental import pallas as pl
from jax.experimental.pallas import tpu as pltpu
from jax.sharding import PartitionSpec as P

HD = 128
F32 = jnp.float32
BF16 = jnp.bfloat16
VMEM = pl.BlockSpec(memory_space=pltpu.VMEM)
ANY = pl.BlockSpec(memory_space=pl.ANY)


def params():
    return pltpu.CompilerParams(vmem_limit_bytes=28 * 1024 * 1024)


def cost(flops, moved):
    return pl.CostEstimate(flops=int(flops), bytes_accessed=int(moved), transcendentals=0)


def copy_all(pairs, sems):
    copies = [pltpu.make_async_copy(source, target, sems.at[i]) for i, (source, target) in enumerate(pairs)]
    for copy in copies:
        copy.start()
    for copy in copies:
        copy.wait()


def pack_kernel(keys_ref, values_ref, kv_out, sems):
    size = keys_ref.shape[1]
    copy_all([(keys_ref, kv_out.at[:, :size]), (values_ref, kv_out.at[:, size:])], sems)


def stage_kernel(sec_ref, q_ref, resid_ref, gain_ref, gate_ref, up_ref, down_ref, *refs):
    q_out, resid_out, gain_out, columns_out, down_out, sems = refs
    half, hidden = q_out.shape[1], gate_ref.shape[1]
    low = pl.multiple_of(sec_ref[0] * half, half)
    rest = pl.multiple_of((1 - sec_ref[0]) * half, half)
    pairs = [
        (q_ref, q_out),
        (resid_ref.at[:, pl.ds(low, half)], resid_out),
        (gain_ref.at[:, pl.ds(low, half)], gain_out.at[:, :half]),
        (gain_ref.at[:, pl.ds(rest, half)], gain_out.at[:, half:]),
        (down_ref.at[:, pl.ds(low, half)], down_out),
    ]
    for c, start in enumerate((low, rest)):
        for n, ref in enumerate((gate_ref, up_ref)):
            target = columns_out.at[c * half : (c + 1) * half, n * hidden : (n + 1) * hidden]
            pairs.append((ref.at[pl.ds(start, half)], target))
    copy_all(pairs, sems)


def attend_kernel(n_pieces, q_ref, resid_ref, gain_ref, pick_ref, *refs):
    kv_refs, stream_ref, outs = refs[:n_pieces], refs[n_pieces], refs[n_pieces + 1 :]
    rows = q_ref.shape[0]
    kv_here = kv_refs[0].shape[1] // (2 * HD)
    group_size = q_ref.shape[1] // HD // kv_here
    factor = math.log2(math.e) / math.sqrt(HD)
    for g in range(kv_here):
        heads = [q_ref[:, (g * group_size + r) * HD : (g * group_size + r + 1) * HD] for r in range(group_size)]
        query = jnp.concatenate(heads, axis=0)
        keys = jnp.concatenate([ref[:, g * HD : (g + 1) * HD] for ref in kv_refs], axis=0)
        values = jnp.concatenate([ref[:, (kv_here + g) * HD : (kv_here + g + 1) * HD] for ref in kv_refs], axis=0)
        scores = lax.dot_general(query, keys, (((1,), (1,)), ((), ())), preferred_element_type=F32)
        raised = jnp.exp2((scores - jnp.max(scores, axis=1, keepdims=True)) * factor)
        total = jnp.sum(raised, axis=1, keepdims=True)
        mixed = jnp.dot(raised.astype(BF16), values, preferred_element_type=F32)
        attended = (mixed / total).astype(BF16).astype(F32)
        for r in range(group_size):
            low = (g * group_size + r) * HD
            stream_ref[:, low : low + HD] = resid_ref[:, low : low + HD].astype(F32) + attended[r * rows : (r + 1) * rows]
    scaled = (stream_ref[...] * gain_ref[:, : q_ref.shape[1]]).astype(BF16)
    for k, out_ref in enumerate(outs):
        out_ref[...] = jnp.dot(pick_ref[k], scaled, preferred_element_type=F32).astype(BF16)


def attend_long(queries, resid, gain, pick, pieces):
    rows, kv_here = queries.shape[0], pieces[0].shape[1] // (2 * HD)
    grouped = queries.reshape(rows, kv_here, -1, HD)
    scale = 1.0 / math.sqrt(HD)
    state = None
    for i in range(0, len(pieces), 8):
        block = jnp.concatenate(pieces[i : i + 8], axis=0).reshape(-1, 2, kv_here, HD)
        scores = jnp.einsum("tgrd,ngd->grtn", grouped, block[:, 0], preferred_element_type=F32) * scale
        top = jnp.max(scores, axis=-1, keepdims=True)
        new_max = top if state is None else jnp.maximum(state[0], top)
        raised = jnp.exp(scores - new_max)
        total = jnp.sum(raised, axis=-1, keepdims=True)
        mixed = jnp.einsum("grtn,ngd->grtd", raised.astype(BF16), block[:, 1], preferred_element_type=F32)
        if state is not None:
            old = jnp.exp(state[0] - new_max)
            total, mixed = state[1] * old + total, state[2] * old + mixed
        state = (new_max, total, mixed)
    attended = (state[2] / state[1]).transpose(2, 0, 1, 3).reshape(rows, -1).astype(BF16)
    stream = resid.astype(F32) + attended.astype(F32)
    scaled = (stream * gain[:, : queries.shape[1]]).astype(BF16)
    return [stream] + [jnp.dot(p, scaled, preferred_element_type=F32).astype(BF16) for p in pick]


def hidden_kernel(width, own_ref, y_ref, x_ref, both_ref, weights_ref, gain_ref, act_ref):
    half, hidden = own_ref.shape[1], act_ref.shape[1]
    total = square = 0.0
    for c, refs in enumerate(((own_ref, y_ref), (x_ref, both_ref))):
        rows = jnp.concatenate([ref[...] for ref in refs], axis=0)
        columns = slice(c * half, (c + 1) * half)
        total = total + jnp.dot(rows, weights_ref[columns, :], preferred_element_type=F32)
        stream = rows.astype(F32) * (1.0 / gain_ref[:, columns])
        square = square + jnp.sum(stream * stream, axis=1, keepdims=True)
    total = total * lax.rsqrt(square / width + 1e-06)
    gate, up = total[:, :hidden], total[:, hidden:]
    act_ref[...] = (gate / (1.0 + jnp.exp(-gate)) * up).astype(BF16)


def down_kernel(rep_ref, own_act, other_act, own_ref, near_ref, far_ref, keep_ref, send_ref, total_ref):
    rows, quarter = keep_ref.shape[0], near_ref.shape[1]
    total_ref[...] = jnp.dot(own_act[...], own_ref[...], preferred_element_type=F32)
    for place, ref in ((rep_ref[0], near_ref), (1 - rep_ref[0], far_ref)):
        columns = pl.ds(pl.multiple_of(place * quarter, quarter), quarter)
        total_ref[:, columns] += jnp.dot(other_act[...], ref[...], preferred_element_type=F32)
    keep_ref[...] = total_ref[:rows]
    send_ref[...] = total_ref[rows:].astype(BF16)


def combine_kernel(stream_ref, high_ref, low_ref, *refs):
    returned, out_ref = refs[:-1], refs[-1]
    rows = [ref[...] for ref in returned]
    weights = [jnp.concatenate([high_ref[k], low_ref[k]], axis=0) for k in range(len(rows))]
    if rows[0].shape[0] % 16 == 0:
        rows, weights = [jnp.concatenate(rows, axis=0)], [jnp.concatenate(weights, axis=1)]
    total = stream_ref[...]
    for weight, block in zip(weights, rows):
        both = jnp.dot(weight, block, preferred_element_type=F32)
        total = total + both[: total.shape[0]] + both[total.shape[0] :]
    out_ref[...] = total.astype(out_ref.dtype)


def near(values):
    return [pltpu.with_memory_space_constraint(v, pltpu.VMEM) for v in values]


def far(values):
    return [pltpu.with_memory_space_constraint(v, pltpu.HBM) for v in values]


def after(value, *others):
    return lax.optimization_barrier((value, *others))[0]


def body(resid, queries, keys, values, norm_gain, expert_ids, gate_weights, w_gate, w_up, w_down):
    rows, width = resid.shape
    half = width // 2
    quarter = half // 2
    n_dev = lax.axis_size("dev")
    n_exp = n_dev // 2
    topk = expert_ids.shape[1]
    cap = max(2, (rows * topk * 5 + 4 * n_exp - 1) // (4 * n_exp))
    hidden = w_gate.shape[2]
    sec = lax.axis_index("sec").astype(jnp.int32)
    rep = lax.axis_index("rep").astype(jnp.int32)
    plane = lax.axis_index("dev").astype(jnp.int32) // 2

    def over_sec(a):
        return lax.ppermute(a, "sec", [(0, 1), (1, 0)])

    def over_rep(a):
        return lax.ppermute(a, "rep", [(0, 1), (1, 0)])

    def over_y(a):
        return lax.ppermute(a, "dev", [(i, i ^ 1) for i in range(n_dev)])

    def over_z(a, k):
        return lax.ppermute(a, "dev", [(i, ((i // 2) ^ k) * 2 + i % 2) for i in range(n_dev)])

    own_kv = pl.pallas_call(
        pack_kernel,
        out_shape=jax.ShapeDtypeStruct((rows, 2 * keys.shape[1]), BF16),
        in_specs=[ANY] * 2,
        out_specs=VMEM,
        scratch_shapes=[pltpu.SemaphoreType.DMA((2,))],
        compiler_params=params(),
        name="pack",
    )(*far([keys, values]))
    planes = [own_kv] + [over_z(own_kv, k) for k in range(1, n_exp)]
    pieces = planes + [over_y(a) for a in planes]

    part = lax.dynamic_slice_in_dim(w_down[0], ((1 - sec) * 2 + rep) * quarter, quarter, 1)
    down_near = over_sec(after(part, planes[1]))

    experts = jnp.arange(n_exp, dtype=jnp.int32)
    onehot = (expert_ids[:, :, None] == experts[None, None, :]).astype(jnp.int32)
    onehot = onehot.reshape(rows * topk, n_exp)
    earlier = jnp.cumsum(onehot, axis=0) - onehot
    slot = jnp.sum(earlier * onehot, axis=1).reshape(rows, topk)
    target = (expert_ids ^ plane) * cap + slot
    placed = target[:, :, None] == jnp.arange(n_exp * cap, dtype=jnp.int32)[None, None, :]
    pick = jnp.sum(placed.astype(F32), axis=1).astype(BF16).T.reshape(n_exp, cap, rows)
    weight = jnp.sum(jnp.where(placed, gate_weights[:, :, None], 0.0), axis=1)
    weight = weight.reshape(rows, n_exp, cap).transpose(1, 0, 2)
    weight_high = weight.astype(BF16)
    weight_low = (weight - weight_high.astype(F32)).astype(BF16)
    smem = pl.BlockSpec(memory_space=pltpu.SMEM)
    staged = pl.pallas_call(
        stage_kernel,
        out_shape=[
            pltpu.VMEM((rows, half), BF16),
            pltpu.VMEM((rows, half), BF16),
            pltpu.VMEM((1, width), F32),
            pltpu.VMEM((width, 2 * hidden), BF16),
            pltpu.VMEM((hidden, half), BF16),
        ],
        in_specs=[smem] + [ANY] * 6,
        out_specs=[VMEM] * 5,
        scratch_shapes=[pltpu.SemaphoreType.DMA((9,))],
        compiler_params=params(),
        name="stage",
    )(sec.reshape(1), *far([queries, resid, norm_gain.reshape(1, width), w_gate[0], w_up[0], w_down[0]]))
    tied = lax.optimization_barrier((pieces[1], pick, weight_high, weight_low, *staged))
    pieces[1], pick, weight_high, weight_low, *staged = tied
    queries, resid, gain, columns, down_own = staged

    if n_dev > 8:
        stream, *sent = attend_long(queries, resid, gain, pick, pieces)
    else:
        n_keys = rows * n_dev
        stream, *sent = pl.pallas_call(
            functools.partial(attend_kernel, len(pieces)),
            in_specs=[VMEM] * (4 + len(pieces)),
            out_specs=[VMEM] * (1 + n_exp),
            out_shape=[jax.ShapeDtypeStruct((rows, half), F32)] + [jax.ShapeDtypeStruct((cap, half), BF16)] * n_exp,
            compiler_params=params(),
            cost_estimate=cost(4 * rows * half * n_keys, n_keys * half * 2),
            name="attend",
        )(queries, resid, gain, pick, *pieces)

    arrived = [sent[0]] + [None] * (n_exp - 1)
    for k in range(1, n_exp):
        arrived[k] = over_z(after(sent[k], arrived[1]) if k == 3 else sent[k], k)
    down_far = over_rep(after(down_near, stream))
    arrived[1] = after(arrived[1], down_far)
    each = max(1, n_exp // 4)
    if each > 1:
        arrived = [jnp.concatenate(arrived[i : i + each], axis=0) for i in range(0, n_exp, each)]

    def plane_gather(number, own):
        if number < 2:
            from_x, from_y = over_sec(own), over_y(own)
            return own, from_y, from_x, over_y(from_x)
        from_y, from_x = over_y(own), over_sec(own)
        return own, from_y, from_x, over_sec(from_y)

    def hidden_of(gathered):
        count = gathered[0].shape[0]
        return pl.pallas_call(
            functools.partial(hidden_kernel, width),
            in_specs=[VMEM] * 6,
            out_specs=VMEM,
            out_shape=jax.ShapeDtypeStruct((2 * count, hidden), BF16),
            compiler_params=params(),
            cost_estimate=cost(8 * count * width * hidden, 4 * width * hidden),
            name="hidden",
        )(*gathered, columns, gain)

    def down_of(act, other_act):
        count = act.shape[0] // 2
        return pl.pallas_call(
            down_kernel,
            in_specs=[smem] + [VMEM] * 5,
            out_specs=[VMEM] * 2,
            out_shape=[jax.ShapeDtypeStruct((count, half), F32), jax.ShapeDtypeStruct((count, half), BF16)],
            scratch_shapes=[pltpu.VMEM((2 * count, half), F32)],
            compiler_params=params(),
            cost_estimate=cost(8 * count * half * hidden, 4 * half * hidden),
            name="down",
        )(rep.reshape(1), act, other_act, down_own, down_near, down_far)

    acts, sends, results, returned = [], [], [], [None] * n_exp
    gathered = [plane_gather(g, block) for g, block in enumerate(arrived)]
    for g, (own, *others) in enumerate(gathered):
        if g > 1:
            own = after(own, sends[g - 2])
        acts.append(hidden_of((own, *others)))
        other_act = over_sec(acts[g])
        if g > 1:
            other_act = after(other_act, results[g - 2])
        keep, send = down_of(acts[g], other_act)
        sends.append(send)
        results.append((keep + over_y(send).astype(F32)).astype(BF16))
        for n, k in enumerate(range(g * each, (g + 1) * each)):
            back = results[g] if each == 1 else results[g][n * cap : (n + 1) * cap]
            returned[k] = back if k == 0 else over_z(back, k)

    return pl.pallas_call(
        combine_kernel,
        out_shape=jax.ShapeDtypeStruct((rows, half), BF16),
        in_specs=[VMEM] * (3 + n_exp),
        out_specs=VMEM,
        compiler_params=params(),
        cost_estimate=cost(4 * n_exp * cap * rows * half, rows * half * 6 + n_exp * cap * half * 2),
        name="combine",
    )(stream, weight_high, weight_low, *returned)


def solution(mesh):
    in_specs = (
        P(("rep", "dev"), None),
        P(("rep", "dev"), "sec"),
        P(("rep", "dev"), "sec"),
        P(("rep", "dev"), "sec"),
        P(),
        P(("rep", "dev"), None),
        P(("rep", "dev"), None),
        P("dev", None, "sec"),
        P("dev", None, "sec"),
        P("dev", "sec", None),
    )
    out_specs = P(("rep", "dev"), "sec")
    return jax.shard_map(body, mesh=mesh, in_specs=in_specs, out_specs=out_specs, check_vma=False)
```

```python
import functools
import math

import jax
import jax.numpy as jnp
from jax import lax
from jax.experimental import pallas as pl
from jax.experimental.pallas import tpu as pltpu
from jax.sharding import PartitionSpec as P

HD = 128
F32 = jnp.float32
BF16 = jnp.bfloat16
VMEM = pl.BlockSpec(memory_space=pltpu.VMEM)
ANY = pl.BlockSpec(memory_space=pl.ANY)


def params():
    return pltpu.CompilerParams(vmem_limit_bytes=28 * 1024 * 1024)


def cost(flops, moved):
    return pl.CostEstimate(flops=int(flops), bytes_accessed=int(moved), transcendentals=0)


def copy_all(pairs, sems):
    copies = [pltpu.make_async_copy(source, target, sems.at[i]) for i, (source, target) in enumerate(pairs)]
    for copy in copies:
        copy.start()
    for copy in copies:
        copy.wait()


def pack_kernel(keys_ref, values_ref, kv_out, sems):
    size = keys_ref.shape[1]
    copy_all([(keys_ref, kv_out.at[:, :size]), (values_ref, kv_out.at[:, size:])], sems)


def stage_kernel(sec_ref, q_ref, resid_ref, gain_ref, gate_ref, up_ref, down_ref, *refs):
    q_out, resid_out, gain_out, columns_out, down_out, sems = refs
    half, hidden = q_out.shape[1], gate_ref.shape[1]
    low = pl.multiple_of(sec_ref[0] * half, half)
    rest = pl.multiple_of((1 - sec_ref[0]) * half, half)
    pairs = [
        (q_ref, q_out),
        (resid_ref.at[:, pl.ds(low, half)], resid_out),
        (gain_ref.at[:, pl.ds(low, half)], gain_out.at[:, :half]),
        (gain_ref.at[:, pl.ds(rest, half)], gain_out.at[:, half:]),
        (down_ref.at[:, pl.ds(low, half)], down_out),
    ]
    for c, start in enumerate((low, rest)):
        for n, ref in enumerate((gate_ref, up_ref)):
            target = columns_out.at[c * half : (c + 1) * half, n * hidden : (n + 1) * hidden]
            pairs.append((ref.at[pl.ds(start, half)], target))
    copy_all(pairs, sems)


def attend_kernel(n_pieces, q_ref, resid_ref, gain_ref, pick_ref, *refs):
    kv_refs, stream_ref, outs = refs[:n_pieces], refs[n_pieces], refs[n_pieces + 1 :]
    rows = q_ref.shape[0]
    kv_here = kv_refs[0].shape[1] // (2 * HD)
    group_size = q_ref.shape[1] // HD // kv_here
    factor = math.log2(math.e) / math.sqrt(HD)
    for g in range(kv_here):
        heads = [q_ref[:, (g * group_size + r) * HD : (g * group_size + r + 1) * HD] for r in range(group_size)]
        query = jnp.concatenate(heads, axis=0)
        keys = jnp.concatenate([ref[:, g * HD : (g + 1) * HD] for ref in kv_refs], axis=0)
        values = jnp.concatenate([ref[:, (kv_here + g) * HD : (kv_here + g + 1) * HD] for ref in kv_refs], axis=0)
        scores = lax.dot_general(query, keys, (((1,), (1,)), ((), ())), preferred_element_type=F32)
        raised = jnp.exp2((scores - jnp.max(scores, axis=1, keepdims=True)) * factor)
        total = jnp.sum(raised, axis=1, keepdims=True)
        mixed = jnp.dot(raised.astype(BF16), values, preferred_element_type=F32)
        attended = (mixed / total).astype(BF16).astype(F32)
        for r in range(group_size):
            low = (g * group_size + r) * HD
            stream_ref[:, low : low + HD] = resid_ref[:, low : low + HD].astype(F32) + attended[r * rows : (r + 1) * rows]
    scaled = (stream_ref[...] * gain_ref[:, : q_ref.shape[1]]).astype(BF16)
    for k, out_ref in enumerate(outs):
        out_ref[...] = jnp.dot(pick_ref[k], scaled, preferred_element_type=F32).astype(BF16)


def attend_long(queries, resid, gain, pick, pieces):
    rows, kv_here = queries.shape[0], pieces[0].shape[1] // (2 * HD)
    grouped = queries.reshape(rows, kv_here, -1, HD)
    scale = 1.0 / math.sqrt(HD)
    state = None
    for i in range(0, len(pieces), 8):
        block = jnp.concatenate(pieces[i : i + 8], axis=0).reshape(-1, 2, kv_here, HD)
        scores = jnp.einsum("tgrd,ngd->grtn", grouped, block[:, 0], preferred_element_type=F32) * scale
        top = jnp.max(scores, axis=-1, keepdims=True)
        new_max = top if state is None else jnp.maximum(state[0], top)
        raised = jnp.exp(scores - new_max)
        total = jnp.sum(raised, axis=-1, keepdims=True)
        mixed = jnp.einsum("grtn,ngd->grtd", raised.astype(BF16), block[:, 1], preferred_element_type=F32)
        if state is not None:
            old = jnp.exp(state[0] - new_max)
            total, mixed = state[1] * old + total, state[2] * old + mixed
        state = (new_max, total, mixed)
    attended = (state[2] / state[1]).transpose(2, 0, 1, 3).reshape(rows, -1).astype(BF16)
    stream = resid.astype(F32) + attended.astype(F32)
    scaled = (stream * gain[:, : queries.shape[1]]).astype(BF16)
    return [stream] + [jnp.dot(p, scaled, preferred_element_type=F32).astype(BF16) for p in pick]


def hidden_kernel(width, own_ref, y_ref, x_ref, both_ref, weights_ref, gain_ref, act_ref):
    half, hidden = own_ref.shape[1], act_ref.shape[1]
    total = square = 0.0
    for c, refs in enumerate(((own_ref, y_ref), (x_ref, both_ref))):
        rows = jnp.concatenate([ref[...] for ref in refs], axis=0)
        columns = slice(c * half, (c + 1) * half)
        total = total + jnp.dot(rows, weights_ref[columns, :], preferred_element_type=F32)
        stream = rows.astype(F32) * (1.0 / gain_ref[:, columns])
        square = square + jnp.sum(stream * stream, axis=1, keepdims=True)
    total = total * lax.rsqrt(square / width + 1e-06)
    gate, up = total[:, :hidden], total[:, hidden:]
    act_ref[...] = (gate / (1.0 + jnp.exp(-gate)) * up).astype(BF16)


def down_kernel(rep_ref, own_act, other_act, own_ref, near_ref, far_ref, keep_ref, send_ref, total_ref):
    rows, quarter = keep_ref.shape[0], near_ref.shape[1]
    total_ref[...] = jnp.dot(own_act[...], own_ref[...], preferred_element_type=F32)
    for place, ref in ((rep_ref[0], near_ref), (1 - rep_ref[0], far_ref)):
        columns = pl.ds(pl.multiple_of(place * quarter, quarter), quarter)
        total_ref[:, columns] += jnp.dot(other_act[...], ref[...], preferred_element_type=F32)
    keep_ref[...] = total_ref[:rows]
    send_ref[...] = total_ref[rows:].astype(BF16)


def combine_kernel(stream_ref, high_ref, low_ref, *refs):
    returned, out_ref = refs[:-1], refs[-1]
    rows = [ref[...] for ref in returned]
    weights = [jnp.concatenate([high_ref[k], low_ref[k]], axis=0) for k in range(len(rows))]
    if rows[0].shape[0] % 16 == 0:
        rows, weights = [jnp.concatenate(rows, axis=0)], [jnp.concatenate(weights, axis=1)]
    total = stream_ref[...]
    for weight, block in zip(weights, rows):
        both = jnp.dot(weight, block, preferred_element_type=F32)
        total = total + both[: total.shape[0]] + both[total.shape[0] :]
    out_ref[...] = total.astype(out_ref.dtype)


def near(values):
    return [pltpu.with_memory_space_constraint(v, pltpu.VMEM) for v in values]


def far(values):
    return [pltpu.with_memory_space_constraint(v, pltpu.HBM) for v in values]


def after(value, *others):
    return lax.optimization_barrier((value, *others))[0]


def body(resid, queries, keys, values, norm_gain, expert_ids, gate_weights, w_gate, w_up, w_down):
    rows, width = resid.shape
    half = width // 2
    quarter = half // 2
    n_dev = lax.axis_size("dev")
    n_exp = n_dev // 2
    topk = expert_ids.shape[1]
    cap = max(2, (rows * topk * 5 + 4 * n_exp - 1) // (4 * n_exp))
    hidden = w_gate.shape[2]
    sec = lax.axis_index("sec").astype(jnp.int32)
    rep = lax.axis_index("rep").astype(jnp.int32)
    plane = lax.axis_index("dev").astype(jnp.int32) // 2

    def over_sec(a):
        return lax.ppermute(a, "sec", [(0, 1), (1, 0)])

    def over_rep(a):
        return lax.ppermute(a, "rep", [(0, 1), (1, 0)])

    def over_y(a):
        return lax.ppermute(a, "dev", [(i, i ^ 1) for i in range(n_dev)])

    def over_z(a, k):
        return lax.ppermute(a, "dev", [(i, ((i // 2) ^ k) * 2 + i % 2) for i in range(n_dev)])

    own_kv = pl.pallas_call(
        pack_kernel,
        out_shape=jax.ShapeDtypeStruct((rows, 2 * keys.shape[1]), BF16),
        in_specs=[ANY] * 2,
        out_specs=VMEM,
        scratch_shapes=[pltpu.SemaphoreType.DMA((2,))],
        compiler_params=params(),
        name="pack",
    )(*far([keys, values]))
    planes = [own_kv] + [over_z(own_kv, k) for k in range(1, n_exp)]
    pieces = planes + [over_y(a) for a in planes]

    part = lax.dynamic_slice_in_dim(w_down[0], ((1 - sec) * 2 + rep) * quarter, quarter, 1)
    down_near = over_sec(after(part, planes[1]))

    experts = jnp.arange(n_exp, dtype=jnp.int32)
    onehot = (expert_ids[:, :, None] == experts[None, None, :]).astype(jnp.int32)
    onehot = onehot.reshape(rows * topk, n_exp)
    earlier = jnp.cumsum(onehot, axis=0) - onehot
    slot = jnp.sum(earlier * onehot, axis=1).reshape(rows, topk)
    target = (expert_ids ^ plane) * cap + slot
    placed = target[:, :, None] == jnp.arange(n_exp * cap, dtype=jnp.int32)[None, None, :]
    pick = jnp.sum(placed.astype(F32), axis=1).astype(BF16).T.reshape(n_exp, cap, rows)
    weight = jnp.sum(jnp.where(placed, gate_weights[:, :, None], 0.0), axis=1)
    weight = weight.reshape(rows, n_exp, cap).transpose(1, 0, 2)
    weight_high = weight.astype(BF16)
    weight_low = (weight - weight_high.astype(F32)).astype(BF16)
    smem = pl.BlockSpec(memory_space=pltpu.SMEM)
    staged = pl.pallas_call(
        stage_kernel,
        out_shape=[
            pltpu.VMEM((rows, half), BF16),
            pltpu.VMEM((rows, half), BF16),
            pltpu.VMEM((1, width), F32),
            pltpu.VMEM((width, 2 * hidden), BF16),
            pltpu.VMEM((hidden, half), BF16),
        ],
        in_specs=[smem] + [ANY] * 6,
        out_specs=[VMEM] * 5,
        scratch_shapes=[pltpu.SemaphoreType.DMA((9,))],
        compiler_params=params(),
        name="stage",
    )(sec.reshape(1), *far([queries, resid, norm_gain.reshape(1, width), w_gate[0], w_up[0], w_down[0]]))
    tied = lax.optimization_barrier((pieces[1], pick, weight_high, weight_low, *staged))
    pieces[1], pick, weight_high, weight_low, *staged = tied
    queries, resid, gain, columns, down_own = staged

    if n_dev > 8:
        stream, *sent = attend_long(queries, resid, gain, pick, pieces)
    else:
        n_keys = rows * n_dev
        stream, *sent = pl.pallas_call(
            functools.partial(attend_kernel, len(pieces)),
            in_specs=[VMEM] * (4 + len(pieces)),
            out_specs=[VMEM] * (1 + n_exp),
            out_shape=[jax.ShapeDtypeStruct((rows, half), F32)] + [jax.ShapeDtypeStruct((cap, half), BF16)] * n_exp,
            compiler_params=params(),
            cost_estimate=cost(2 * rows * half * n_keys, n_keys * half),
            name="attend",
        )(queries, resid, gain, pick, *pieces)

    arrived = [sent[0]] + [None] * (n_exp - 1)
    for k in range(1, n_exp):
        arrived[k] = over_z(after(sent[k], arrived[1]) if k == 3 else sent[k], k)
    down_far = over_rep(after(down_near, stream))
    arrived[1] = after(arrived[1], down_far)
    each = max(1, n_exp // 4)
    if each > 1:
        arrived = [jnp.concatenate(arrived[i : i + each], axis=0) for i in range(0, n_exp, each)]

    def plane_gather(number, own):
        if number < 2:
            from_x, from_y = over_sec(own), over_y(own)
            return own, from_y, from_x, over_y(from_x)
        from_y, from_x = over_y(own), over_sec(own)
        return own, from_y, from_x, over_sec(from_y)

    def hidden_of(gathered):
        count = gathered[0].shape[0]
        return pl.pallas_call(
            functools.partial(hidden_kernel, width),
            in_specs=[VMEM] * 6,
            out_specs=VMEM,
            out_shape=jax.ShapeDtypeStruct((2 * count, hidden), BF16),
            compiler_params=params(),
            cost_estimate=cost(4 * count * width * hidden, 2 * width * hidden),
            name="hidden",
        )(*gathered, columns, gain)

    def down_of(act, other_act):
        count = act.shape[0] // 2
        return pl.pallas_call(
            down_kernel,
            in_specs=[smem] + [VMEM] * 5,
            out_specs=[VMEM] * 2,
            out_shape=[jax.ShapeDtypeStruct((count, half), F32), jax.ShapeDtypeStruct((count, half), BF16)],
            scratch_shapes=[pltpu.VMEM((2 * count, half), F32)],
            compiler_params=params(),
            cost_estimate=cost(4.8 * count * half * hidden, 2.4 * half * hidden),
            name="down",
        )(rep.reshape(1), act, other_act, down_own, down_near, down_far)

    acts, sends, results, returned = [], [], [], [None] * n_exp
    gathered = [plane_gather(g, block) for g, block in enumerate(arrived)]
    for g, (own, *others) in enumerate(gathered):
        if g > 1:
            own = after(own, sends[g - 2])
        acts.append(hidden_of((own, *others)))
        other_act = over_sec(acts[g])
        if g > 1:
            other_act = after(other_act, results[g - 2])
        keep, send = down_of(acts[g], other_act)
        sends.append(send)
        results.append((keep + over_y(send).astype(F32)).astype(BF16))
        for n, k in enumerate(range(g * each, (g + 1) * each)):
            back = results[g] if each == 1 else results[g][n * cap : (n + 1) * cap]
            returned[k] = back if k == 0 else over_z(back, k)

    return pl.pallas_call(
        combine_kernel,
        out_shape=jax.ShapeDtypeStruct((rows, half), BF16),
        in_specs=[VMEM] * (3 + n_exp),
        out_specs=VMEM,
        compiler_params=params(),
        cost_estimate=cost(4 * n_exp * cap * rows * half, rows * half * 6 + n_exp * cap * half * 2),
        name="combine",
    )(stream, weight_high, weight_low, *returned)


def solution(mesh):
    in_specs = (
        P(("rep", "dev"), None),
        P(("rep", "dev"), "sec"),
        P(("rep", "dev"), "sec"),
        P(("rep", "dev"), "sec"),
        P(),
        P(("rep", "dev"), None),
        P(("rep", "dev"), None),
        P("dev", None, "sec"),
        P("dev", None, "sec"),
        P("dev", "sec", None),
    )
    out_specs = P(("rep", "dev"), "sec")
    return jax.shard_map(body, mesh=mesh, in_specs=in_specs, out_specs=out_specs, check_vma=False)
```
